32 devices in a mesh: ctx: 16 (over z, y, core), tp: 2 (over x).
Axes of the slice: x: 2, y: 2, z: 4, core: 2. Of those that a mesh axis runs over, the one named last changes fastest.
Arguments:
- tokens: bfloat16 [5120, 6144], P('ctx', 'tp'), may hold values from -6 to 6
- norm_gain_vector: bfloat16 [6144], P('tp'), may hold values from 0.099609375 to 1.8984375
- keys: bfloat16 [5120, 3072], P('ctx', 'tp'), may hold values from -67 to 67
- values: bfloat16 [5120, 3072], P('ctx', 'tp'), may hold values from -6 to 6
- query_frozen_weight: bfloat16 [6144, 3072], P(None, 'tp'), may hold values from -0.078125 to 0.078125
- output_frozen_weight: bfloat16 [3072, 6144], P('tp'), may hold values from -2 to 2
- query_update_first: bfloat16 [16, 6144, 64], P('ctx'), may hold values from -0.078125 to 0.078125
- query_update_second: bfloat16 [16, 64, 3072], P('ctx', None, 'tp'), may hold values from -0.75 to 0.75
- output_update_first: bfloat16 [16, 3072, 64], P('ctx', 'tp'), may hold values from -0.109375 to 0.109375
- output_update_second: bfloat16 [16, 64, 6144], P('ctx'), may hold values from -6 to 6
- owners: int32 [4], replicated, may hold values from 0 to 15
- frame_block_number: int32 [80], replicated, may hold values from 0 to 19, never falling along the last dimension, each value on 1 to 8 neighbouring positions
Outputs:
- mixed: bfloat16 [5120, 6144], P('ctx', 'tp')
The draws below stay inside these ranges and needn't reach their ends.
Inputs may be any that keep to these rules, and one draw needn't show every extreme that they name: `frame_block_number`: never falls along the frames; every block holds 1 to 8 frames, one exactly 8.
All inputs are finite; a program needn't handle non-finite values.
Results may differ from the reference program's by a relative error of at most 0.02.
The reference program's roundings to bfloat16 on the way count: a program that leaves them out, or rounds other values in their place, can miss the bound.
Values may be sent and summed in bfloat16 or wider, within the bound.
A program may use at most 192 MiB of HBM per device.

```python
import math
import jax
import jax.numpy as jnp
import numpy as np
from jax import lax

MODEL_WIDTH = 6144
HEADS = 24
HS = 128
LOWRANK_SIZE = 64
FTOK = 64
SEQ = 5120
QUERY_FEATURES = 3072
FRAMES = 80
N_CTX = 16


def draw_keys(key, part):
    key = jax.random.fold_in(key, 11)
    first_key, second_key = jax.random.split(key, 2)
    leading = jnp.clip(jax.random.normal(first_key, (SEQ // 2, QUERY_FEATURES), jnp.float32), -4.0, 4.0)
    partner = jnp.clip(jax.random.normal(second_key, (SEQ // 2, QUERY_FEATURES), jnp.float32), -4.0, 4.0)
    paired = jnp.stack([leading, leading + 0.3 * partner], axis=1)
    return paired.reshape(SEQ, QUERY_FEATURES).astype(jnp.bfloat16)


def with_ends(values, key, low, largest):
    longest = values.shape.index(max(values.shape))
    spots = []
    for shift in (0, 1):
        where = [jax.random.randint(jax.random.fold_in(key, axis), (), 0, length) for axis, length in enumerate(values.shape)]
        where[longest] = (where[longest] + shift) % values.shape[longest]
        spots.append(tuple(where))
    return values.at[spots[0]].set(low).at[spots[1]].set(largest)


def levels(own_key, shape, shards, smallest, top_value):
    level = 1.0
    for position, shards_of in shards:
        draws = jax.random.uniform(jax.random.fold_in(jax.random.fold_in(own_key, 6), position), (shards_of,), jnp.float32, smallest / len(shards), top_value / len(shards))
        level = level * jnp.repeat(jnp.exp(draws), shape[position] // shards_of).reshape((-1,) + (1,) * (len(shape) - 1 - position))
    return level


def length_profile(count, total, most, slope):
    portions = [(1 << 20) // math.isqrt(grade ** slope) + 1 for grade in range(2, count + 1)]
    rest, counts = total - most - (count - 1), [1] * (count - 1)
    while rest > 0:
        movable = [i for i in range(count - 1) if counts[i] < most]
        pool, budget = sum([portions[i] for i in movable]), rest
        for i in movable:
            addition = min(most - counts[i], max(1, budget * portions[i] // pool), rest)
            counts[i] = counts[i] + addition
            rest = rest - addition
    return np.array([most] + counts)


def ragged_sizes(key, count, total, limit, slope):
    if count == 2:
        one = jax.random.randint(key, (), max(1, total - limit), min(limit, total - 1) + 1)
        return jnp.stack([one, total - one])
    tallies = jnp.asarray(length_profile(count, total, limit, slope), jnp.int32)
    couples = (count - 1) // 2
    donor, receiver = tallies[1:1 + 2 * couples:2], tallies[2:2 + 2 * couples:2]
    slack = jnp.minimum(donor - 1, limit - receiver)
    shifted = jax.random.randint(jax.random.fold_in(key, 1), (couples,), 0, 1 << 20) % (slack + 1)
    tallies = tallies.at[1:1 + 2 * couples:2].set(donor - shifted).at[2:2 + 2 * couples:2].set(receiver + shifted)
    return tallies[jax.random.permutation(jax.random.fold_in(key, 2), count)]


def centred(rng, extent, width, reach, cuts=(), dtype=jnp.bfloat16):
    entries = width * jax.random.normal(rng, extent, jnp.float32)
    if cuts:
        entries = entries * levels(rng, extent, cuts, -0.22, 0.18)
    return jnp.clip(entries, -reach, reach).astype(dtype)


def setup_inputs(seed: int = 0) -> dict:
    key_of = jax.random.split(jax.random.key(seed), 13)
    tokens = centred(key_of[0], (SEQ, MODEL_WIDTH), 1.0, 6.0, ((0, 16), (1, 2)))
    norm_gain_vector = jnp.clip(1.0 + 0.18 * jax.random.normal(key_of[1], (MODEL_WIDTH,), jnp.float32), 0.099609375, 1.8984375).astype(jnp.bfloat16)
    keys = draw_keys(jax.random.fold_in(key_of[12], 71), 0)
    values = centred(key_of[3], (SEQ, QUERY_FEATURES), 1.0, 6.0, ((0, 16), (1, 2)))
    query_frozen_weight = centred(key_of[4], (MODEL_WIDTH, QUERY_FEATURES), MODEL_WIDTH ** -0.5, 0.078125, ((1, 2),))
    output_frozen_weight = centred(key_of[5], (QUERY_FEATURES, MODEL_WIDTH), 8 ** -0.5, 2.0, ((0, 2),))
    query_update_first = centred(key_of[6], (N_CTX, MODEL_WIDTH, LOWRANK_SIZE), MODEL_WIDTH ** -0.5, 0.078125, ((0, 16),))
    query_update_second = centred(key_of[7], (N_CTX, LOWRANK_SIZE, QUERY_FEATURES), LOWRANK_SIZE ** -0.5, 0.75, ((0, 16), (2, 2)))
    output_update_first = centred(key_of[8], (N_CTX, QUERY_FEATURES, LOWRANK_SIZE), QUERY_FEATURES ** -0.5, 0.109375, ((0, 16), (1, 2)))
    output_update_second = centred(key_of[9], (N_CTX, LOWRANK_SIZE, MODEL_WIDTH), 1 ** -0.5, 6.0, ((0, 16),))
    owners = with_ends(jax.random.randint(key_of[10], (4,), 0, N_CTX), jax.random.fold_in(key_of[10], 1), 0, N_CTX - 1).astype(jnp.int32)
    frame_block_number = jnp.searchsorted(jnp.cumsum(ragged_sizes(key_of[11], FRAMES // 4, FRAMES, 8, 1)), jnp.arange(FRAMES), side="right").astype(jnp.int32)
    return dict(tokens=tokens, norm_gain_vector=norm_gain_vector, keys=keys, values=values, query_frozen_weight=query_frozen_weight, output_frozen_weight=output_frozen_weight, query_update_first=query_update_first, query_update_second=query_update_second, output_update_first=output_update_first, output_update_second=output_update_second, owners=owners, frame_block_number=frame_block_number)


norm_eps = 1e-06
masked_score = -1e+30

def reference(tokens, norm_gain_vector, keys, values, query_frozen_weight, output_frozen_weight, query_update_first, query_update_second, output_update_first, output_update_second, owners, frame_block_number):
    features = tokens.astype(jnp.float32)
    mean_square = lax.optimization_barrier(jnp.mean(features * features, axis=-1, keepdims=True))
    normed = (features * lax.rsqrt(mean_square + norm_eps) * norm_gain_vector.astype(jnp.float32)).astype(jnp.bfloat16)
    query_down_factor = lax.dynamic_index_in_dim(query_update_first, owners[0], 0, keepdims=False)
    query_up_factor = lax.dynamic_index_in_dim(query_update_second, owners[1], 0, keepdims=False)
    output_down_factor = lax.dynamic_index_in_dim(output_update_first, owners[2], 0, keepdims=False)
    output_up_factor = lax.dynamic_index_in_dim(output_update_second, owners[3], 0, keepdims=False)
    query_merged = (query_frozen_weight.astype(jnp.float32) + jnp.dot(query_down_factor, query_up_factor, preferred_element_type=jnp.float32)).astype(jnp.bfloat16)
    out_merged = (output_frozen_weight.astype(jnp.float32) + jnp.dot(output_down_factor, output_up_factor, preferred_element_type=jnp.float32)).astype(jnp.bfloat16)
    queries = jnp.dot(normed, query_merged, preferred_element_type=jnp.float32).astype(jnp.bfloat16)
    token_block = jnp.repeat(frame_block_number, FTOK, total_repeat_length=SEQ)
    visible = token_block[None, :] <= token_block[:, None]

    def per_head(operands):
        head_queries, head_keys, head_values = operands
        scores = jnp.dot(head_queries, head_keys.T, preferred_element_type=jnp.float32) * HS ** (-0.5)
        scores = jnp.where(visible, scores, masked_score)
        top = lax.optimization_barrier(jnp.max(scores, axis=-1, keepdims=True))
        weights = jnp.where(visible, jnp.exp(scores - top), 0.0)
        total = lax.optimization_barrier(jnp.sum(weights, axis=-1, keepdims=True))
        summed = jnp.dot(weights.astype(jnp.bfloat16), head_values, preferred_element_type=jnp.float32)
        return summed / total

    def split_heads(matrix):
        return matrix.reshape(SEQ, HEADS, HS).transpose(1, 0, 2)
    attended = lax.map(per_head, (split_heads(queries), split_heads(keys), split_heads(values)))
    attended = attended.transpose(1, 0, 2).reshape(SEQ, QUERY_FEATURES).astype(jnp.bfloat16)
    return jnp.dot(attended, out_merged, preferred_element_type=jnp.float32).astype(jnp.bfloat16)
```

```python
import functools

import jax
import jax.numpy as jnp
from jax import lax
from jax.experimental import pallas as pl
from jax.experimental.pallas import tpu as pltpu
from jax.sharding import PartitionSpec as P

HS = 128
FTOK = 64
norm_eps = 1e-06
masked_score = -1e30
LOG2E = 1.4426950408889634


def swap(x, bit):
    n = lax.axis_size("ctx")
    return lax.ppermute(x, "ctx", [(i, i ^ bit) for i in range(n)])


def fetch_pair(down, up, down_owner, up_owner):
    n = lax.axis_size("ctx")
    me = lax.axis_index("ctx")
    cols = down.shape[0]
    buf = jnp.concatenate([down.T, up], axis=1)
    owner = jnp.where(jnp.arange(buf.shape[1]) < cols, down_owner, up_owner)[None, :]
    halved = []
    bit = 1
    while bit < n:
        high = (me & bit) != 0
        if bit <= 2:
            half = buf.shape[1] // 2
            low_part, high_part = buf[:, :half], buf[:, half:]
            received = swap(jnp.where(high, low_part, high_part), bit)
            kept = jnp.where(high, high_part, low_part)
            owner = jnp.where(high, owner[:, half:], owner[:, :half])
            halved.append(bit)
        else:
            received = swap(buf, bit)
            kept = buf
        buf = jnp.where((owner & bit) == (me & bit), kept, received)
        bit *= 2
    for bit in reversed(halved):
        high = (me & bit) != 0
        other = swap(buf, bit)
        buf = jnp.concatenate(
            [jnp.where(high, other, buf), jnp.where(high, buf, other)], axis=1
        )
    return buf[:, :cols], buf[:, cols:]


def merge_weight(base, down_t, up):
    product = lax.dot_general(
        down_t, up, (((0,), (0,)), ((), ())), preferred_element_type=jnp.float32
    )
    return (base.astype(jnp.float32) + product).astype(jnp.bfloat16)


def attention_kernel(groups, ranks, heads, rows, *refs):
    n = groups * ranks
    info, kid, qid = refs[:3]
    q_in = refs[3 : 3 + groups]
    kv_in = refs[3 + groups : 3 + groups + n]
    outs = refs[3 + groups + n : 3 + 2 * groups + n]
    q_buf, kv_buf, o_buf, top, total, acc, q_sem, kv_sem, o_sem = refs[3 + 2 * groups + n :]
    loads = [pltpu.make_async_copy(q_in[i], q_buf.at[i], q_sem.at[i]) for i in range(groups)]
    loads += [pltpu.make_async_copy(kv_in[i], kv_buf.at[i], kv_sem.at[i]) for i in range(n)]
    for load in loads:
        load.start()
    for load in loads:
        load.wait()
    my_group, my_rank = info[2 * groups], info[2 * groups + 1]
    rate = HS ** (-0.5) * LOG2E

    def group_body(g, carry):
        top[...] = jnp.full(top.shape, masked_score, jnp.float32)
        total[...] = jnp.zeros(total.shape, jnp.float32)
        acc[...] = jnp.zeros(acc.shape, jnp.float32)

        def chunk(c, masked):
            first = 2 * c
            slots = []
            for r in (first, first + 1):
                slots.append((r // ranks ^ my_group) * ranks + (r % ranks ^ my_rank))
            if masked:
                seen = kid[c] <= qid[g]
            for h in range(heads):
                cut = slice(h * HS, (h + 1) * HS)
                k = jnp.concatenate([kv_buf[s, :rows, cut] for s in slots], axis=0)
                v = jnp.concatenate([kv_buf[s, rows:, cut] for s in slots], axis=0)
                scores = lax.dot_general(
                    q_buf[g, :, cut], k, (((1,), (1,)), ((), ())),
                    preferred_element_type=jnp.float32,
                )
                if masked:
                    scores = jnp.where(seen, scores, masked_score)
                old = top[h]
                new = jnp.maximum(old, jnp.max(scores, axis=1, keepdims=True))
                weights = jnp.exp2((scores - new[:, :1]) * rate)
                factor = jnp.exp2((old - new) * rate)
                top[h] = new
                total[h] = total[h] * factor + jnp.sum(weights, axis=1, keepdims=True)
                acc[h] = acc[h] * factor + jnp.dot(
                    weights.astype(jnp.bfloat16), v, preferred_element_type=jnp.float32
                )

        def plain(c, carry):
            chunk(c, False)
            return carry

        def edge(c, carry):
            chunk(c, True)
            return carry

        lax.fori_loop(0, info[g], plain, 0)
        lax.fori_loop(info[g], info[groups + g], edge, 0)
        for h in range(heads):
            o_buf[g, :, h * HS : (h + 1) * HS] = (acc[h] / total[h]).astype(jnp.bfloat16)
        return carry

    lax.fori_loop(0, groups, group_body, 0)
    stores = [pltpu.make_async_copy(o_buf.at[i], outs[i], o_sem.at[i]) for i in range(groups)]
    for store in stores:
        store.start()
    for store in stores:
        store.wait()


def attend(q_parts, kv_parts, groups, ranks, frame_block_number):
    rows, width = q_parts[0].shape
    heads = width // HS
    n = groups * ranks
    me = lax.axis_index("ctx")
    my_group, my_rank = me // ranks, me % ranks
    frames = rows // FTOK
    chunk_frames = 2 * frames
    blocks = frame_block_number.reshape(n, frames)
    q_ranks = (jnp.arange(groups) ^ my_group) * ranks + my_rank
    own = blocks[q_ranks]
    full = jnp.sum(frame_block_number[None, :] <= own[:, :1], axis=1) // chunk_frames
    some = jnp.sum(frame_block_number[None, :] <= own[:, -1:], axis=1)
    some = (some + chunk_frames - 1) // chunk_frames
    info = jnp.concatenate([full, some, jnp.stack([my_group, my_rank])]).astype(jnp.int32)
    kid = jnp.repeat(frame_block_number, FTOK).reshape(n // 2, 1, 2 * rows)
    qid = jnp.repeat(own, FTOK, axis=1).reshape(groups, rows, 1)
    bf16, f32 = jnp.bfloat16, jnp.float32
    any_spec = pl.BlockSpec(memory_space=pl.ANY)
    return pl.pallas_call(
        functools.partial(attention_kernel, groups, ranks, heads, rows),
        out_shape=[jax.ShapeDtypeStruct((rows, width), bf16)] * groups,
        in_specs=[
            pl.BlockSpec(memory_space=pltpu.SMEM),
            pl.BlockSpec(memory_space=pltpu.VMEM),
            pl.BlockSpec(memory_space=pltpu.VMEM),
        ]
        + [any_spec] * (groups + n),
        out_specs=[any_spec] * groups,
        scratch_shapes=[
            pltpu.VMEM((groups, rows, width), bf16),
            pltpu.VMEM((n, 2 * rows, width), bf16),
            pltpu.VMEM((groups, rows, width), bf16),
            pltpu.VMEM((heads, rows, HS), f32),
            pltpu.VMEM((heads, rows, HS), f32),
            pltpu.VMEM((heads, rows, HS), f32),
            pltpu.SemaphoreType.DMA((groups,)),
            pltpu.SemaphoreType.DMA((n,)),
            pltpu.SemaphoreType.DMA((groups,)),
        ],
        compiler_params=pltpu.CompilerParams(vmem_limit_bytes=48 * 2**20),
        cost_estimate=pl.CostEstimate(
            flops=2 * groups * rows * n * rows * width,
            bytes_accessed=(2 * n + 2 * groups) * rows * width * 2,
            transcendentals=groups * rows * n * rows * heads // 2,
        ),
        name="block_attention",
    )(info, kid, qid, *q_parts, *kv_parts)


def shards(
    tokens,
    norm_gain_vector,
    keys,
    values,
    query_frozen_weight,
    output_frozen_weight,
    query_update_first,
    query_update_second,
    output_update_first,
    output_update_second,
    owners,
    frame_block_number,
):
    n, tp = lax.axis_size("ctx"), lax.axis_size("tp")
    me, mine = lax.axis_index("ctx"), lax.axis_index("tp")
    local_heads = keys.shape[1] // HS
    groups = next(g for g in (4, 2, 1) if local_heads % g == 0 and n % (2 * g) == 0)
    ranks = n // groups
    width = keys.shape[1] // groups
    my_group = me // ranks

    def columns(x, step):
        return lax.dynamic_slice_in_dim(x, (my_group ^ step) * width, width, 1)

    whole = lax.all_gather(tokens, "tp", axis=1, tiled=True)
    gain = lax.all_gather(norm_gain_vector, "tp", axis=0, tiled=True)
    query_down_t, query_up = fetch_pair(
        query_update_first[0], query_update_second[0], owners[0], owners[1]
    )

    kv_parts = []
    for step in range(groups):
        part = jnp.concatenate([columns(keys, step), columns(values, step)], axis=0)
        if step:
            part = swap(part, step * ranks)
        have = {0: part}
        bit = ranks // 2
        while bit:
            have.update({j | bit: swap(x, bit) for j, x in list(have.items())})
            bit //= 2
        kv_parts += [have[j] for j in range(ranks)]

    features = whole.astype(jnp.float32)
    mean_square = jnp.mean(features * features, axis=-1, keepdims=True)
    normed = (features * lax.rsqrt(mean_square + norm_eps) * gain.astype(jnp.float32)).astype(
        jnp.bfloat16
    )
    query_merged = merge_weight(query_frozen_weight, query_down_t, query_up)
    queries = jnp.dot(normed, query_merged, preferred_element_type=jnp.float32).astype(jnp.bfloat16)

    q_parts = []
    for step in range(groups):
        part = columns(queries, step)
        q_parts.append(swap(part, step * ranks) if step else part)

    out_down_t, out_up = fetch_pair(
        output_update_first[0], output_update_second[0], owners[2], owners[3]
    )
    out_merged = merge_weight(output_frozen_weight, out_down_t, out_up)

    o_parts = attend(q_parts, kv_parts, groups, ranks, frame_block_number)
    stacked = jnp.stack([swap(o, i * ranks) if i else o for i, o in enumerate(o_parts)])
    attended = jnp.concatenate(
        [lax.dynamic_index_in_dim(stacked, my_group ^ g, 0, keepdims=False) for g in range(groups)],
        axis=1,
    )
    if tp != 2:
        partial_value = jnp.dot(attended, out_merged, preferred_element_type=jnp.float32)
        return lax.psum_scatter(
            partial_value.astype(jnp.bfloat16), "tp", scatter_dimension=1, tiled=True
        )
    half = out_merged.shape[1] // 2
    pieces = 4
    step = half // pieces
    received = []
    for i in range(pieces):
        theirs = lax.dynamic_slice_in_dim(out_merged, (1 - mine) * half + i * step, step, 1)
        product = jnp.dot(attended, theirs, preferred_element_type=jnp.float32)
        received.append(lax.ppermute(product.astype(jnp.bfloat16), "tp", [(0, 1), (1, 0)]))
    own = lax.dynamic_slice_in_dim(out_merged, mine * half, half, 1)
    product = jnp.dot(attended, own, preferred_element_type=jnp.float32)
    return jnp.concatenate(
        [
            (product[:, i * step : (i + 1) * step] + received[i].astype(jnp.float32)).astype(
                jnp.bfloat16
            )
            for i in range(pieces)
        ],
        axis=1,
    )


def solution(mesh):
    in_specs = (
        P("ctx", "tp"),
        P("tp"),
        P("ctx", "tp"),
        P("ctx", "tp"),
        P(None, "tp"),
        P("tp", None),
        P("ctx", None, None),
        P("ctx", None, "tp"),
        P("ctx", "tp", None),
        P("ctx", None, None),
        P(),
        P(),
    )
    out_specs = P("ctx", "tp")
    return jax.shard_map(shards, mesh=mesh, in_specs=in_specs, out_specs=out_specs, check_vma=False)
```

```python
import functools

import jax
import jax.numpy as jnp
from jax import lax
from jax.experimental import pallas as pl
from jax.experimental.pallas import tpu as pltpu
from jax.sharding import PartitionSpec as P

HS = 128
FTOK = 64
norm_eps = 1e-06
masked_score = -1e30
LOG2E = 1.4426950408889634


def swap(x, bit):
    n = lax.axis_size("ctx")
    return lax.ppermute(x, "ctx", [(i, i ^ bit) for i in range(n)])


def fetch_pair(down, up, down_owner, up_owner, hold=None):
    n = lax.axis_size("ctx")
    me = lax.axis_index("ctx")
    cols = down.shape[0]
    buf = jnp.concatenate([down.T, up], axis=1)
    owner = jnp.where(jnp.arange(buf.shape[1]) < cols, down_owner, up_owner)[None, :]
    halved = []
    bit = 1
    while bit < n:
        high = (me & bit) != 0
        if bit <= 2:
            half = buf.shape[1] // 2
            low_part, high_part = buf[:, :half], buf[:, half:]
            received = swap(jnp.where(high, low_part, high_part), bit)
            kept = jnp.where(high, high_part, low_part)
            owner = jnp.where(high, owner[:, half:], owner[:, :half])
            halved.append(bit)
        else:
            if hold is not None:
                buf, _ = lax.optimization_barrier((buf, hold))
                hold = None
            received = swap(buf, bit)
            kept = buf
        buf = jnp.where((owner & bit) == (me & bit), kept, received)
        bit *= 2
    part = buf
    for bit in reversed(halved):
        high = (me & bit) != 0
        other = swap(buf, bit)
        buf = jnp.concatenate(
            [jnp.where(high, other, buf), jnp.where(high, buf, other)], axis=1
        )
    return buf[:, :cols], buf[:, cols:], part


def merge_weight(base, down_t, up):
    product = lax.dot_general(
        down_t, up, (((0,), (0,)), ((), ())), preferred_element_type=jnp.float32
    )
    return (base.astype(jnp.float32) + product).astype(jnp.bfloat16)


def attention_kernel(n, heads, rows, *refs):
    info, kid, qid, q_in = refs[:4]
    kv_in = refs[4 : 4 + n]
    out, kv_buf, top, total, acc, kv_sem = refs[4 + n :]
    for i in range(n):
        pltpu.make_async_copy(kv_in[i], kv_buf.at[i], kv_sem.at[i]).start()
    top[...] = jnp.full(top.shape, masked_score, jnp.float32)
    total[...] = jnp.zeros(total.shape, jnp.float32)
    acc[...] = jnp.zeros(acc.shape, jnp.float32)
    mine = info[2]
    rate = HS ** (-0.5) * LOG2E

    def slots_of(c):
        return (2 * c) ^ mine, (2 * c + 1) ^ mine

    def arrived(c):
        for s in slots_of(c):
            pltpu.make_async_copy(kv_buf.at[s], kv_buf.at[s], kv_sem.at[s]).wait()

    def chunk(c, masked):
        slots = slots_of(c)
        if masked:
            seen = kid[c] <= qid[...]

        def score(h):
            cut = slice(h * HS, (h + 1) * HS)
            k = jnp.concatenate([kv_buf[s, :rows, cut] for s in slots], axis=0)
            scores = lax.dot_general(
                q_in[:, cut], k, (((1,), (1,)), ((), ())), preferred_element_type=jnp.float32
            )
            return jnp.where(seen, scores, masked_score) if masked else scores

        following = score(0)
        for h in range(heads):
            scores = following
            if h + 1 < heads:
                following = score(h + 1)
            cut = slice(h * HS, (h + 1) * HS)
            v = jnp.concatenate([kv_buf[s, rows:, cut] for s in slots], axis=0)
            old = top[h]
            new = jnp.maximum(old, jnp.max(scores, axis=1, keepdims=True))
            weights = jnp.exp2((scores - new[:, :1]) * rate)
            factor = jnp.exp2((old - new) * rate)
            lanes = weights[:, :HS]
            for j in range(1, 2 * rows // HS):
                lanes = lanes + weights[:, j * HS : (j + 1) * HS]
            top[h] = new
            total[h] = total[h] * factor + lanes
            acc[h] = acc[h] * factor + jnp.dot(
                weights.astype(jnp.bfloat16), v, preferred_element_type=jnp.float32
            )

    def plain(c, carry):
        arrived(c)
        chunk(c, False)
        return carry

    def edge(c, carry):
        arrived(c)
        chunk(c, True)
        return carry

    def unused(c, carry):
        arrived(c)
        return carry

    lax.fori_loop(0, info[0], plain, 0)
    lax.fori_loop(info[0], info[1], edge, 0)
    lax.fori_loop(info[1], n // 2, unused, 0)
    for h in range(heads):
        out[:, h * HS : (h + 1) * HS] = (
            acc[h] / jnp.sum(total[h], axis=1, keepdims=True)
        ).astype(jnp.bfloat16)


def attend(q_part, kv_parts, q_rank, frame_block_number):
    rows, width = q_part.shape
    heads = width // HS
    n = len(kv_parts)
    frames = rows // FTOK
    chunk_frames = 2 * frames
    own = lax.dynamic_slice_in_dim(frame_block_number, q_rank * frames, frames, 0)
    full = jnp.sum(frame_block_number <= own[0]) // chunk_frames
    some = (jnp.sum(frame_block_number <= own[-1]) + chunk_frames - 1) // chunk_frames
    info = jnp.stack([full, some, lax.axis_index("ctx")]).astype(jnp.int32)
    kid = jnp.repeat(frame_block_number, FTOK).reshape(n // 2, 1, 2 * rows)
    qid = jnp.repeat(own, FTOK).reshape(rows, 1)
    bf16, f32 = jnp.bfloat16, jnp.float32
    vmem = pl.BlockSpec(memory_space=pltpu.VMEM)
    return pl.pallas_call(
        functools.partial(attention_kernel, n, heads, rows),
        out_shape=jax.ShapeDtypeStruct((rows, width), bf16),
        in_specs=[pl.BlockSpec(memory_space=pltpu.SMEM), vmem, vmem, vmem]
        + [pl.BlockSpec(memory_space=pl.ANY)] * n,
        out_specs=vmem,
        scratch_shapes=[
            pltpu.VMEM((n, 2 * rows, width), bf16),
            pltpu.VMEM((heads, rows, HS), f32),
            pltpu.VMEM((heads, rows, HS), f32),
            pltpu.VMEM((heads, rows, HS), f32),
            pltpu.SemaphoreType.DMA((n,)),
        ],
        compiler_params=pltpu.CompilerParams(vmem_limit_bytes=40 * 2**20),
        cost_estimate=pl.CostEstimate(
            flops=4 * rows * n * rows * width,
            bytes_accessed=(2 * n + 2) * rows * width * 2,
            transcendentals=rows * n * rows * heads // 2,
        ),
        name="block_attention",
    )(info, kid, qid, q_part, *kv_parts)


def shards(
    tokens,
    norm_gain_vector,
    keys,
    values,
    query_frozen_weight,
    output_frozen_weight,
    query_update_first,
    query_update_second,
    output_update_first,
    output_update_second,
    owners,
    frame_block_number,
):
    n, tp = lax.axis_size("ctx"), lax.axis_size("tp")
    me, mine = lax.axis_index("ctx"), lax.axis_index("tp")
    local_heads = keys.shape[1] // HS
    groups = next(g for g in (4, 2, 1) if local_heads % g == 0 and n % (2 * g) == 0)
    ranks = n // groups
    width = keys.shape[1] // groups
    my_group = me // ranks

    def columns(x, step):
        return lax.dynamic_slice_in_dim(x, (my_group ^ step) * width, width, 1)

    gain = lax.all_gather(norm_gain_vector, "tp", axis=0, tiled=True)
    query_down_t, query_up, fetched = fetch_pair(
        query_update_first[0], query_update_second[0], owners[0], owners[1]
    )
    whole = lax.all_gather(tokens, "tp", axis=1, tiled=True)

    held_keys, held_values, _ = lax.optimization_barrier((keys, values, fetched))
    kv_parts = []
    for step in range(groups):
        part = jnp.concatenate([columns(held_keys, step), columns(held_values, step)], axis=0)
        if step:
            part = swap(part, step * ranks)
        have = {0: part}
        bit = ranks // 2
        while bit:
            have.update({j | bit: swap(x, bit) for j, x in list(have.items())})
            bit //= 2
        kv_parts += [have[j] for j in range(ranks)]

    features = whole.astype(jnp.float32)
    mean_square = jnp.mean(features * features, axis=-1, keepdims=True)
    normed = (features * lax.rsqrt(mean_square + norm_eps) * gain.astype(jnp.float32)).astype(
        jnp.bfloat16
    )
    query_merged = merge_weight(query_frozen_weight, query_down_t, query_up)
    queries = jnp.dot(normed, query_merged, preferred_element_type=jnp.float32).astype(jnp.bfloat16)

    q_parts = []
    for step in range(groups):
        part = columns(queries, step)
        q_parts.append(swap(part, step * ranks) if step else part)

    out_down_t, out_up, _ = fetch_pair(
        output_update_first[0],
        output_update_second[0],
        owners[2],
        owners[3],
        hold=tuple(q_parts),
    )

    order = list(range(1, groups)) + [0]
    o_parts = [None] * groups
    gate = None
    for step in order:
        q_part = q_parts[step]
        if gate is not None:
            q_part, _ = lax.optimization_barrier((q_part, gate))
        gate = attend(q_part, kv_parts, (my_group ^ step) * ranks + me % ranks, frame_block_number)
        o_parts[step] = swap(gate, step * ranks) if step else gate
    out_merged = merge_weight(output_frozen_weight, out_down_t, out_up)
    stacked = jnp.stack(o_parts)
    attended = jnp.concatenate(
        [lax.dynamic_index_in_dim(stacked, my_group ^ g, 0, keepdims=False) for g in range(groups)],
        axis=1,
    )
    if tp != 2:
        partial_value = jnp.dot(attended, out_merged, preferred_element_type=jnp.float32)
        return lax.psum_scatter(
            partial_value.astype(jnp.bfloat16), "tp", scatter_dimension=1, tiled=True
        )
    half = out_merged.shape[1] // 2
    pieces = 4
    step = half // pieces
    received = []
    for i in range(pieces):
        theirs = lax.dynamic_slice_in_dim(out_merged, (1 - mine) * half + i * step, step, 1)
        product = jnp.dot(attended, theirs, preferred_element_type=jnp.float32)
        received.append(lax.ppermute(product.astype(jnp.bfloat16), "tp", [(0, 1), (1, 0)]))
    own = lax.dynamic_slice_in_dim(out_merged, mine * half, half, 1)
    product = jnp.dot(attended, own, preferred_element_type=jnp.float32)
    return jnp.concatenate(
        [
            (product[:, i * step : (i + 1) * step] + received[i].astype(jnp.float32)).astype(
                jnp.bfloat16
            )
            for i in range(pieces)
        ],
        axis=1,
    )


def solution(mesh):
    in_specs = (
        P("ctx", "tp"),
        P("tp"),
        P("ctx", "tp"),
        P("ctx", "tp"),
        P(None, "tp"),
        P("tp", None),
        P("ctx", None, None),
        P("ctx", None, "tp"),
        P("ctx", "tp", None),
        P("ctx", None, None),
        P(),
        P(),
    )
    out_specs = P("ctx", "tp")
    return jax.shard_map(shards, mesh=mesh, in_specs=in_specs, out_specs=out_specs, check_vma=False)
```

```python
import functools

import jax
import jax.numpy as jnp
from jax import lax
from jax.experimental import pallas as pl
from jax.experimental.pallas import tpu as pltpu
from jax.sharding import PartitionSpec as P

HS = 128
FTOK = 64
norm_eps = 1e-06
masked_score = -1e30
LOG2E = 1.4426950408889634


def swap(x, bit):
    n = lax.axis_size("ctx")
    return lax.ppermute(x, "ctx", [(i, i ^ bit) for i in range(n)])


def fetch_pair(down, up, down_owner, up_owner, hold=None):
    n = lax.axis_size("ctx")
    me = lax.axis_index("ctx")
    cols = down.shape[0]
    buf = jnp.concatenate([down.T, up], axis=1)
    if hold is not None:
        buf, _ = lax.optimization_barrier((buf, hold))
    owner = jnp.where(jnp.arange(buf.shape[1]) < cols, down_owner, up_owner)[None, :]
    halved = []
    bit = 1
    while bit < n:
        high = (me & bit) != 0
        if bit <= 2:
            half = buf.shape[1] // 2
            low_part, high_part = buf[:, :half], buf[:, half:]
            received = swap(jnp.where(high, low_part, high_part), bit)
            kept = jnp.where(high, high_part, low_part)
            owner = jnp.where(high, owner[:, half:], owner[:, :half])
            halved.append(bit)
        else:
            received = swap(buf, bit)
            kept = buf
        buf = jnp.where((owner & bit) == (me & bit), kept, received)
        if bit <= 2:
            after_halving = buf
        bit *= 2
    part = buf
    for bit in reversed(halved):
        high = (me & bit) != 0
        other = swap(buf, bit)
        buf = jnp.concatenate(
            [jnp.where(high, other, buf), jnp.where(high, buf, other)], axis=1
        )
    return buf[:, :cols], buf[:, cols:], after_halving, part


def merge_weight(base, down_t, up):
    product = lax.dot_general(
        down_t, up, (((0,), (0,)), ((), ())), preferred_element_type=jnp.float32
    )
    return (base.astype(jnp.float32) + product).astype(jnp.bfloat16)


def attention_kernel(n, heads, rows, *refs):
    info, kid, qid, q_in = refs[:4]
    kv_in = refs[4 : 4 + n]
    out, kv_buf, top, total, acc, kv_sem = refs[4 + n :]
    for i in range(n):
        pltpu.make_async_copy(kv_in[i], kv_buf.at[i], kv_sem.at[i]).start()
    top[...] = jnp.full(top.shape, masked_score, jnp.float32)
    total[...] = jnp.zeros(total.shape, jnp.float32)
    acc[...] = jnp.zeros(acc.shape, jnp.float32)
    mine = info[2]
    rate = HS ** (-0.5) * LOG2E

    def slots_of(c):
        return (2 * c) ^ mine, (2 * c + 1) ^ mine

    def arrived(c):
        for s in slots_of(c):
            pltpu.make_async_copy(kv_buf.at[s], kv_buf.at[s], kv_sem.at[s]).wait()

    def chunk(c, masked):
        slots = slots_of(c)
        if masked:
            seen = kid[c] <= qid[...]

        def score(h):
            cut = slice(h * HS, (h + 1) * HS)
            k = jnp.concatenate([kv_buf[s, :rows, cut] for s in slots], axis=0)
            scores = lax.dot_general(
                q_in[:, cut], k, (((1,), (1,)), ((), ())), preferred_element_type=jnp.float32
            )
            return jnp.where(seen, scores, masked_score) if masked else scores

        following = score(0)
        for h in range(heads):
            scores = following
            if h + 1 < heads:
                following = score(h + 1)
            cut = slice(h * HS, (h + 1) * HS)
            v = jnp.concatenate([kv_buf[s, rows:, cut] for s in slots], axis=0)
            old = top[h]
            new = jnp.maximum(old, jnp.max(scores, axis=1, keepdims=True))
            weights = jnp.exp2((scores - new[:, :1]) * rate)
            factor = jnp.exp2((old - new) * rate)
            lanes = weights[:, :HS]
            for j in range(1, 2 * rows // HS):
                lanes = lanes + weights[:, j * HS : (j + 1) * HS]
            top[h] = new
            total[h] = total[h] * factor + lanes
            acc[h] = acc[h] * factor + jnp.dot(
                weights.astype(jnp.bfloat16), v, preferred_element_type=jnp.float32
            )

    def plain(c, carry):
        arrived(c)
        chunk(c, False)
        return carry

    def edge(c, carry):
        arrived(c)
        chunk(c, True)
        return carry

    def unused(c, carry):
        arrived(c)
        return carry

    lax.fori_loop(0, info[0], plain, 0)
    lax.fori_loop(info[0], info[1], edge, 0)
    lax.fori_loop(info[1], n // 2, unused, 0)
    for h in range(heads):
        out[:, h * HS : (h + 1) * HS] = (
            acc[h] / jnp.sum(total[h], axis=1, keepdims=True)
        ).astype(jnp.bfloat16)


def attend(q_part, kv_parts, q_rank, frame_block_number):
    rows, width = q_part.shape
    heads = width // HS
    n = len(kv_parts)
    frames = rows // FTOK
    chunk_frames = 2 * frames
    own = lax.dynamic_slice_in_dim(frame_block_number, q_rank * frames, frames, 0)
    full = jnp.sum(frame_block_number <= own[0]) // chunk_frames
    some = (jnp.sum(frame_block_number <= own[-1]) + chunk_frames - 1) // chunk_frames
    info = jnp.stack([full, some, lax.axis_index("ctx")]).astype(jnp.int32)
    kid = jnp.repeat(frame_block_number, FTOK).reshape(n // 2, 1, 2 * rows)
    qid = jnp.repeat(own, FTOK).reshape(rows, 1)
    bf16, f32 = jnp.bfloat16, jnp.float32
    vmem = pl.BlockSpec(memory_space=pltpu.VMEM)
    return pl.pallas_call(
        functools.partial(attention_kernel, n, heads, rows),
        out_shape=jax.ShapeDtypeStruct((rows, width), bf16),
        in_specs=[pl.BlockSpec(memory_space=pltpu.SMEM), vmem, vmem, vmem]
        + [pl.BlockSpec(memory_space=pl.ANY)] * n,
        out_specs=vmem,
        scratch_shapes=[
            pltpu.VMEM((n, 2 * rows, width), bf16),
            pltpu.VMEM((heads, rows, HS), f32),
            pltpu.VMEM((heads, rows, HS), f32),
            pltpu.VMEM((heads, rows, HS), f32),
            pltpu.SemaphoreType.DMA((n,)),
        ],
        compiler_params=pltpu.CompilerParams(vmem_limit_bytes=40 * 2**20),
        cost_estimate=pl.CostEstimate(
            flops=4 * rows * n * rows * width,
            bytes_accessed=(2 * n + 2) * rows * width * 2,
            transcendentals=rows * n * rows * heads // 2,
        ),
        name="block_attention",
    )(info, kid, qid, q_part, *kv_parts)


def shards(
    tokens,
    norm_gain_vector,
    keys,
    values,
    query_frozen_weight,
    output_frozen_weight,
    query_update_first,
    query_update_second,
    output_update_first,
    output_update_second,
    owners,
    frame_block_number,
):
    n, tp = lax.axis_size("ctx"), lax.axis_size("tp")
    me, mine = lax.axis_index("ctx"), lax.axis_index("tp")
    local_heads = keys.shape[1] // HS
    groups = next(g for g in (4, 2, 1) if local_heads % g == 0 and n % (2 * g) == 0)
    ranks = n // groups
    width = keys.shape[1] // groups
    my_group = me // ranks

    def columns(x, step):
        return lax.dynamic_slice_in_dim(x, (my_group ^ step) * width, width, 1)

    gain = lax.all_gather(norm_gain_vector, "tp", axis=0, tiled=True)
    query_down_t, query_up, after_halving, fetched = fetch_pair(
        query_update_first[0], query_update_second[0], owners[0], owners[1]
    )
    if tp == 2:
        other = lax.ppermute(tokens, "tp", [(0, 1), (1, 0)])
        whole = jnp.concatenate(
            [jnp.where(mine == 0, tokens, other), jnp.where(mine == 0, other, tokens)], axis=1
        )
    else:
        whole = lax.all_gather(tokens, "tp", axis=1, tiled=True)

    kv_parts = []
    for step in range(groups):
        part = jnp.concatenate([columns(keys, step), columns(values, step)], axis=0)
        if step == 0:
            part, _ = lax.optimization_barrier((part, after_halving))
        elif step < groups - 1:
            part, _ = lax.optimization_barrier((part, fetched))
        if step:
            part = swap(part, step * ranks)
        have = {0: part}
        bit = ranks // 2
        while bit:
            have.update({j | bit: swap(x, bit) for j, x in list(have.items())})
            bit //= 2
        kv_parts += [have[j] for j in range(ranks)]

    features = whole.astype(jnp.float32)
    mean_square = jnp.mean(features * features, axis=-1, keepdims=True)
    normed = (features * lax.rsqrt(mean_square + norm_eps) * gain.astype(jnp.float32)).astype(
        jnp.bfloat16
    )
    query_merged = merge_weight(query_frozen_weight, query_down_t, query_up)
    queries = jnp.dot(normed, query_merged, preferred_element_type=jnp.float32).astype(jnp.bfloat16)

    q_parts = []
    for step in range(groups):
        part = columns(queries, step)
        q_parts.append(swap(part, step * ranks) if step else part)

    out_down_t, out_up, _, _ = fetch_pair(
        output_update_first[0], output_update_second[0], owners[2], owners[3], hold=fetched
    )
    out_merged = merge_weight(output_frozen_weight, out_down_t, out_up)

    order = list(range(1, groups)) + [0]
    o_parts = [None] * groups
    gate = out_merged
    for step in order:
        q_part = q_parts[step]
        q_part, _ = lax.optimization_barrier((q_part, gate))
        gate = attend(q_part, kv_parts, (my_group ^ step) * ranks + me % ranks, frame_block_number)
        o_parts[step] = swap(gate, step * ranks) if step else gate
    stacked = jnp.stack(o_parts)
    attended = jnp.concatenate(
        [lax.dynamic_index_in_dim(stacked, my_group ^ g, 0, keepdims=False) for g in range(groups)],
        axis=1,
    )
    if tp != 2:
        partial_value = jnp.dot(attended, out_merged, preferred_element_type=jnp.float32)
        return lax.psum_scatter(
            partial_value.astype(jnp.bfloat16), "tp", scatter_dimension=1, tiled=True
        )
    half = out_merged.shape[1] // 2
    pieces = 4
    step = half // pieces
    received = []
    for i in range(pieces):
        theirs = lax.dynamic_slice_in_dim(out_merged, (1 - mine) * half + i * step, step, 1)
        product = jnp.dot(attended, theirs, preferred_element_type=jnp.float32)
        received.append(lax.ppermute(product.astype(jnp.bfloat16), "tp", [(0, 1), (1, 0)]))
    own = lax.dynamic_slice_in_dim(out_merged, mine * half, half, 1)
    product = jnp.dot(attended, own, preferred_element_type=jnp.float32)
    return jnp.concatenate(
        [
            (product[:, i * step : (i + 1) * step] + received[i].astype(jnp.float32)).astype(
                jnp.bfloat16
            )
            for i in range(pieces)
        ],
        axis=1,
    )


def solution(mesh):
    in_specs = (
        P("ctx", "tp"),
        P("tp"),
        P("ctx", "tp"),
        P("ctx", "tp"),
        P(None, "tp"),
        P("tp", None),
        P("ctx", None, None),
        P("ctx", None, "tp"),
        P("ctx", "tp", None),
        P("ctx", None, None),
        P(),
        P(),
    )
    out_specs = P("ctx", "tp")
    return jax.shard_map(shards, mesh=mesh, in_specs=in_specs, out_specs=out_specs, check_vma=False)
```

```python
import functools

import jax
import jax.numpy as jnp
from jax import lax
from jax.experimental import pallas as pl
from jax.experimental.pallas import tpu as pltpu
from jax.sharding import PartitionSpec as P

HS = 128
FTOK = 64
norm_eps = 1e-06
masked_score = -1e30
LOG2E = 1.4426950408889634


def swap(x, bit):
    n = lax.axis_size("ctx")
    return lax.ppermute(x, "ctx", [(i, i ^ bit) for i in range(n)])


def fetch_pair(down, up, down_owner, up_owner, hold=None):
    n = lax.axis_size("ctx")
    me = lax.axis_index("ctx")
    cols = down.shape[0]
    buf = jnp.concatenate([down.T, up], axis=1)
    owner = jnp.where(jnp.arange(buf.shape[1]) < cols, down_owner, up_owner)[None, :]
    halved = []
    bit = 1
    while bit < n:
        high = (me & bit) != 0
        if bit <= 2:
            half = buf.shape[1] // 2
            low_part, high_part = buf[:, :half], buf[:, half:]
            received = swap(jnp.where(high, low_part, high_part), bit)
            kept = jnp.where(high, high_part, low_part)
            owner = jnp.where(high, owner[:, half:], owner[:, :half])
            halved.append(bit)
        else:
            if hold is not None:
                buf, _ = lax.optimization_barrier((buf, hold))
                hold = None
            received = swap(buf, bit)
            kept = buf
        buf = jnp.where((owner & bit) == (me & bit), kept, received)
        if bit <= 2:
            after_halving = buf
        bit *= 2
    part = buf
    for bit in reversed(halved):
        high = (me & bit) != 0
        other = swap(buf, bit)
        buf = jnp.concatenate(
            [jnp.where(high, other, buf), jnp.where(high, buf, other)], axis=1
        )
    return buf[:, :cols], buf[:, cols:], after_halving, part


def merge_weight(base, down_t, up):
    product = lax.dot_general(
        down_t, up, (((0,), (0,)), ((), ())), preferred_element_type=jnp.float32
    )
    return (base.astype(jnp.float32) + product).astype(jnp.bfloat16)


def attention_kernel(n, heads, rows, *refs):
    info, kid, qid, q_in = refs[:4]
    kv_in = refs[4 : 4 + n]
    out, kv_buf, top, total, acc, kv_sem = refs[4 + n :]
    for i in range(n):
        pltpu.make_async_copy(kv_in[i], kv_buf.at[i], kv_sem.at[i]).start()
    top[...] = jnp.full(top.shape, masked_score, jnp.float32)
    total[...] = jnp.zeros(total.shape, jnp.float32)
    acc[...] = jnp.zeros(acc.shape, jnp.float32)
    mine = info[2]
    rate = HS ** (-0.5) * LOG2E

    def slots_of(c):
        return (2 * c) ^ mine, (2 * c + 1) ^ mine

    def arrived(c):
        for s in slots_of(c):
            pltpu.make_async_copy(kv_buf.at[s], kv_buf.at[s], kv_sem.at[s]).wait()

    def chunk(c, masked):
        slots = slots_of(c)
        if masked:
            seen = kid[c] <= qid[...]

        def score(h):
            cut = slice(h * HS, (h + 1) * HS)
            k = jnp.concatenate([kv_buf[s, :rows, cut] for s in slots], axis=0)
            scores = lax.dot_general(
                q_in[:, cut], k, (((1,), (1,)), ((), ())), preferred_element_type=jnp.float32
            )
            return jnp.where(seen, scores, masked_score) if masked else scores

        following = score(0)
        for h in range(heads):
            scores = following
            if h + 1 < heads:
                following = score(h + 1)
            cut = slice(h * HS, (h + 1) * HS)
            v = jnp.concatenate([kv_buf[s, rows:, cut] for s in slots], axis=0)
            old = top[h]
            new = jnp.maximum(old, jnp.max(scores, axis=1, keepdims=True))
            weights = jnp.exp2((scores - new[:, :1]) * rate)
            factor = jnp.exp2((old - new) * rate)
            lanes = weights[:, :HS]
            for j in range(1, 2 * rows // HS):
                lanes = lanes + weights[:, j * HS : (j + 1) * HS]
            top[h] = new
            total[h] = total[h] * factor + lanes
            acc[h] = acc[h] * factor + jnp.dot(
                weights.astype(jnp.bfloat16), v, preferred_element_type=jnp.float32
            )

    def plain(c, carry):
        arrived(c)
        chunk(c, False)
        return carry

    def edge(c, carry):
        arrived(c)
        chunk(c, True)
        return carry

    def unused(c, carry):
        arrived(c)
        return carry

    lax.fori_loop(0, info[0], plain, 0)
    lax.fori_loop(info[0], info[1], edge, 0)
    lax.fori_loop(info[1], n // 2, unused, 0)
    for h in range(heads):
        out[:, h * HS : (h + 1) * HS] = (
            acc[h] / jnp.sum(total[h], axis=1, keepdims=True)
        ).astype(jnp.bfloat16)


def attend(q_part, kv_parts, q_rank, frame_block_number):
    rows, width = q_part.shape
    heads = width // HS
    n = len(kv_parts)
    frames = rows // FTOK
    chunk_frames = 2 * frames
    own = lax.dynamic_slice_in_dim(frame_block_number, q_rank * frames, frames, 0)
    full = jnp.sum(frame_block_number <= own[0]) // chunk_frames
    some = (jnp.sum(frame_block_number <= own[-1]) + chunk_frames - 1) // chunk_frames
    info = jnp.stack([full, some, lax.axis_index("ctx")]).astype(jnp.int32)
    kid = jnp.repeat(frame_block_number, FTOK).reshape(n // 2, 1, 2 * rows)
    qid = jnp.repeat(own, FTOK).reshape(rows, 1)
    bf16, f32 = jnp.bfloat16, jnp.float32
    vmem = pl.BlockSpec(memory_space=pltpu.VMEM)
    return pl.pallas_call(
        functools.partial(attention_kernel, n, heads, rows),
        out_shape=jax.ShapeDtypeStruct((rows, width), bf16),
        in_specs=[pl.BlockSpec(memory_space=pltpu.SMEM), vmem, vmem, vmem]
        + [pl.BlockSpec(memory_space=pl.ANY)] * n,
        out_specs=vmem,
        scratch_shapes=[
            pltpu.VMEM((n, 2 * rows, width), bf16),
            pltpu.VMEM((heads, rows, HS), f32),
            pltpu.VMEM((heads, rows, HS), f32),
            pltpu.VMEM((heads, rows, HS), f32),
            pltpu.SemaphoreType.DMA((n,)),
        ],
        compiler_params=pltpu.CompilerParams(vmem_limit_bytes=40 * 2**20),
        cost_estimate=pl.CostEstimate(
            flops=4 * rows * n * rows * width,
            bytes_accessed=(2 * n + 2) * rows * width * 2,
            transcendentals=rows * n * rows * heads // 2,
        ),
        name="block_attention",
    )(info, kid, qid, q_part, *kv_parts)


def shards(
    tokens,
    norm_gain_vector,
    keys,
    values,
    query_frozen_weight,
    output_frozen_weight,
    query_update_first,
    query_update_second,
    output_update_first,
    output_update_second,
    owners,
    frame_block_number,
):
    n, tp = lax.axis_size("ctx"), lax.axis_size("tp")
    me, mine = lax.axis_index("ctx"), lax.axis_index("tp")
    local_heads = keys.shape[1] // HS
    groups = next(g for g in (4, 2, 1) if local_heads % g == 0 and n % (2 * g) == 0)
    ranks = n // groups
    width = keys.shape[1] // groups
    my_group = me // ranks

    def columns(x, step):
        return lax.dynamic_slice_in_dim(x, (my_group ^ step) * width, width, 1)

    query_down_t, query_up, after_halving, fetched = fetch_pair(
        query_update_first[0], query_update_second[0], owners[0], owners[1]
    )
    if tp == 2:

        def both(x):
            other = lax.ppermute(x, "tp", [(0, 1), (1, 0)])
            return jnp.concatenate(
                [jnp.where(mine == 0, x, other), jnp.where(mine == 0, other, x)], axis=1
            )

        whole, gain = both(tokens), both(norm_gain_vector[None, :])
    else:
        gain = lax.all_gather(norm_gain_vector[None, :], "tp", axis=1, tiled=True)
        whole = lax.all_gather(tokens, "tp", axis=1, tiled=True)

    kv_parts = []
    early = []
    for step in range(groups):
        part = jnp.concatenate([columns(keys, step), columns(values, step)], axis=0)
        if step == 0:
            part, _ = lax.optimization_barrier((part, after_halving))
        elif step < groups - 1:
            part, _ = lax.optimization_barrier((part, fetched))
        if step:
            part = swap(part, step * ranks)
        have = {0: part}
        bit = ranks // 2
        while bit:
            have.update({j | bit: swap(x, bit) for j, x in list(have.items())})
            bit //= 2
        kv_parts += [have[j] for j in range(ranks)]
        if step in (0, groups - 1):
            early.append(have[ranks // 2])
        else:
            early.append(part)

    query_down_t, _ = lax.optimization_barrier((query_down_t, early))
    features = whole.astype(jnp.float32)
    mean_square = jnp.mean(features * features, axis=-1, keepdims=True)
    normed = (features * lax.rsqrt(mean_square + norm_eps) * gain.astype(jnp.float32)).astype(
        jnp.bfloat16
    )
    query_merged = merge_weight(query_frozen_weight, query_down_t, query_up)
    queries = jnp.dot(normed, query_merged, preferred_element_type=jnp.float32).astype(jnp.bfloat16)

    q_parts = []
    for step in range(groups):
        part = columns(queries, step)
        q_parts.append(swap(part, step * ranks) if step else part)

    out_down_t, out_up, _, _ = fetch_pair(
        output_update_first[0], output_update_second[0], owners[2], owners[3], hold=queries
    )
    out_merged = merge_weight(output_frozen_weight, out_down_t, out_up)

    order = list(range(1, groups)) + [0]
    o_parts = [None] * groups
    gate = None
    for step in order:
        q_part = q_parts[step]
        if gate is not None:
            q_part, _ = lax.optimization_barrier((q_part, (gate, out_merged) if step == 0 else gate))
        gate = attend(q_part, kv_parts, (my_group ^ step) * ranks + me % ranks, frame_block_number)
        o_parts[step] = swap(gate, step * ranks) if step else gate
    stacked = jnp.stack(o_parts)
    attended = jnp.concatenate(
        [lax.dynamic_index_in_dim(stacked, my_group ^ g, 0, keepdims=False) for g in range(groups)],
        axis=1,
    )
    if tp != 2:
        partial_value = jnp.dot(attended, out_merged, preferred_element_type=jnp.float32)
        return lax.psum_scatter(
            partial_value.astype(jnp.bfloat16), "tp", scatter_dimension=1, tiled=True
        )
    half = out_merged.shape[1] // 2
    pieces = 6
    step = half // pieces
    received = []
    for i in range(pieces):
        theirs = lax.dynamic_slice_in_dim(out_merged, (1 - mine) * half + i * step, step, 1)
        product = jnp.dot(attended, theirs, preferred_element_type=jnp.float32)
        received.append(lax.ppermute(product.astype(jnp.bfloat16), "tp", [(0, 1), (1, 0)]))
    own = lax.dynamic_slice_in_dim(out_merged, mine * half, half, 1)
    product = jnp.dot(attended, own, preferred_element_type=jnp.float32)
    return jnp.concatenate(
        [
            (product[:, i * step : (i + 1) * step] + received[i].astype(jnp.float32)).astype(
                jnp.bfloat16
            )
            for i in range(pieces)
        ],
        axis=1,
    )


def solution(mesh):
    in_specs = (
        P("ctx", "tp"),
        P("tp"),
        P("ctx", "tp"),
        P("ctx", "tp"),
        P(None, "tp"),
        P("tp", None),
        P("ctx", None, None),
        P("ctx", None, "tp"),
        P("ctx", "tp", None),
        P("ctx", None, None),
        P(),
        P(),
    )
    out_specs = P("ctx", "tp")
    return jax.shard_map(shards, mesh=mesh, in_specs=in_specs, out_specs=out_specs, check_vma=False)
```

```python
import functools

import jax
import jax.numpy as jnp
from jax import lax
from jax.experimental import pallas as pl
from jax.experimental.pallas import tpu as pltpu
from jax.sharding import PartitionSpec as P

HS = 128
FTOK = 64
norm_eps = 1e-06
masked_score = -1e30
LOG2E = 1.4426950408889634


def swap(x, bit):
    n = lax.axis_size("ctx")
    return lax.ppermute(x, "ctx", [(i, i ^ bit) for i in range(n)])


def fetch_pair(down, up, down_owner, up_owner, hold=None):
    n = lax.axis_size("ctx")
    me = lax.axis_index("ctx")
    cols = down.shape[0]
    buf = jnp.concatenate([down.T, up], axis=1)
    owner = jnp.where(jnp.arange(buf.shape[1]) < cols, down_owner, up_owner)[None, :]
    halved = []
    bit = 1
    while bit < n:
        high = (me & bit) != 0
        if bit <= 2:
            half = buf.shape[1] // 2
            low_part, high_part = buf[:, :half], buf[:, half:]
            received = swap(jnp.where(high, low_part, high_part), bit)
            kept = jnp.where(high, high_part, low_part)
            owner = jnp.where(high, owner[:, half:], owner[:, :half])
            halved.append(bit)
        else:
            if hold is not None:
                buf, _ = lax.optimization_barrier((buf, hold))
                hold = None
            received = swap(buf, bit)
            kept = buf
        buf = jnp.where((owner & bit) == (me & bit), kept, received)
        if bit <= 2:
            after_halving = buf
        bit *= 2
    part = buf
    for bit in reversed(halved):
        high = (me & bit) != 0
        other = swap(buf, bit)
        buf = jnp.concatenate(
            [jnp.where(high, other, buf), jnp.where(high, buf, other)], axis=1
        )
    return buf[:, :cols], buf[:, cols:], after_halving, part


def merge_weight(base, down_t, up):
    product = lax.dot_general(
        down_t, up, (((0,), (0,)), ((), ())), preferred_element_type=jnp.float32
    )
    return (base.astype(jnp.float32) + product).astype(jnp.bfloat16)


def attention_kernel(n, heads, rows, *refs):
    info, kid, qid, q_in = refs[:4]
    kv_in = refs[4 : 4 + n]
    out, kv_buf, top, total, acc, kv_sem = refs[4 + n :]
    for i in range(n):
        pltpu.make_async_copy(kv_in[i], kv_buf.at[i], kv_sem.at[i]).start()
    top[...] = jnp.full(top.shape, masked_score, jnp.float32)
    total[...] = jnp.zeros(total.shape, jnp.float32)
    acc[...] = jnp.zeros(acc.shape, jnp.float32)
    mine = info[2]
    rate = HS ** (-0.5) * LOG2E

    def slots_of(c):
        return (2 * c) ^ mine, (2 * c + 1) ^ mine

    def arrived(c):
        for s in slots_of(c):
            pltpu.make_async_copy(kv_buf.at[s], kv_buf.at[s], kv_sem.at[s]).wait()

    def chunk(c, masked):
        slots = slots_of(c)
        if masked:
            seen = kid[c] <= qid[...]

        def score(h):
            cut = slice(h * HS, (h + 1) * HS)
            k = jnp.concatenate([kv_buf[s, :rows, cut] for s in slots], axis=0)
            scores = lax.dot_general(
                q_in[:, cut], k, (((1,), (1,)), ((), ())), preferred_element_type=jnp.float32
            )
            return jnp.where(seen, scores, masked_score) if masked else scores

        following = score(0)
        for h in range(heads):
            scores = following
            if h + 1 < heads:
                following = score(h + 1)
            cut = slice(h * HS, (h + 1) * HS)
            v = jnp.concatenate([kv_buf[s, rows:, cut] for s in slots], axis=0)
            old = top[h]
            new = jnp.maximum(old, jnp.max(scores, axis=1, keepdims=True))
            weights = jnp.exp2((scores - new[:, :1]) * rate)
            factor = jnp.exp2((old - new) * rate)
            lanes = weights[:, :HS]
            for j in range(1, 2 * rows // HS):
                lanes = lanes + weights[:, j * HS : (j + 1) * HS]
            top[h] = new
            total[h] = total[h] * factor + lanes
            acc[h] = acc[h] * factor + jnp.dot(
                weights.astype(jnp.bfloat16), v, preferred_element_type=jnp.float32
            )

    def plain(c, carry):
        arrived(c)
        chunk(c, False)
        return carry

    def edge(c, carry):
        arrived(c)
        chunk(c, True)
        return carry

    def unused(c, carry):
        arrived(c)
        return carry

    lax.fori_loop(0, info[0], plain, 0)
    lax.fori_loop(info[0], info[1], edge, 0)
    lax.fori_loop(info[1], n // 2, unused, 0)
    for h in range(heads):
        out[:, h * HS : (h + 1) * HS] = (
            acc[h] / jnp.sum(total[h], axis=1, keepdims=True)
        ).astype(jnp.bfloat16)


def attend(q_part, kv_parts, q_rank, frame_block_number):
    rows, width = q_part.shape
    heads = width // HS
    n = len(kv_parts)
    frames = rows // FTOK
    chunk_frames = 2 * frames
    own = lax.dynamic_slice_in_dim(frame_block_number, q_rank * frames, frames, 0)
    full = jnp.sum(frame_block_number <= own[0]) // chunk_frames
    some = (jnp.sum(frame_block_number <= own[-1]) + chunk_frames - 1) // chunk_frames
    info = jnp.stack([full, some, lax.axis_index("ctx")]).astype(jnp.int32)
    kid = jnp.repeat(frame_block_number, FTOK).reshape(n // 2, 1, 2 * rows)
    qid = jnp.repeat(own, FTOK).reshape(rows, 1)
    bf16, f32 = jnp.bfloat16, jnp.float32
    vmem = pl.BlockSpec(memory_space=pltpu.VMEM)
    return pl.pallas_call(
        functools.partial(attention_kernel, n, heads, rows),
        out_shape=jax.ShapeDtypeStruct((rows, width), bf16),
        in_specs=[pl.BlockSpec(memory_space=pltpu.SMEM), vmem, vmem, vmem]
        + [pl.BlockSpec(memory_space=pl.ANY)] * n,
        out_specs=vmem,
        scratch_shapes=[
            pltpu.VMEM((n, 2 * rows, width), bf16),
            pltpu.VMEM((heads, rows, HS), f32),
            pltpu.VMEM((heads, rows, HS), f32),
            pltpu.VMEM((heads, rows, HS), f32),
            pltpu.SemaphoreType.DMA((n,)),
        ],
        compiler_params=pltpu.CompilerParams(vmem_limit_bytes=40 * 2**20),
        cost_estimate=pl.CostEstimate(
            flops=4 * rows * n * rows * width,
            bytes_accessed=(2 * n + 2) * rows * width * 2,
            transcendentals=rows * n * rows * heads // 2,
        ),
        name="block_attention",
    )(info, kid, qid, q_part, *kv_parts)


def shards(
    tokens,
    norm_gain_vector,
    keys,
    values,
    query_frozen_weight,
    output_frozen_weight,
    query_update_first,
    query_update_second,
    output_update_first,
    output_update_second,
    owners,
    frame_block_number,
):
    n, tp = lax.axis_size("ctx"), lax.axis_size("tp")
    me, mine = lax.axis_index("ctx"), lax.axis_index("tp")
    local_heads = keys.shape[1] // HS
    groups = next(g for g in (4, 2, 1) if local_heads % g == 0 and n % (2 * g) == 0)
    ranks = n // groups
    width = keys.shape[1] // groups
    my_group = me // ranks

    def columns(x, step):
        return lax.dynamic_slice_in_dim(x, (my_group ^ step) * width, width, 1)

    query_down_t, query_up, after_halving, fetched = fetch_pair(
        query_update_first[0], query_update_second[0], owners[0], owners[1]
    )
    if tp == 2:

        def both(x):
            other = lax.ppermute(x, "tp", [(0, 1), (1, 0)])
            return jnp.concatenate(
                [jnp.where(mine == 0, x, other), jnp.where(mine == 0, other, x)], axis=1
            )

        whole, gain = both(tokens), both(norm_gain_vector[None, :])
    else:
        gain = lax.all_gather(norm_gain_vector[None, :], "tp", axis=1, tiled=True)
        whole = lax.all_gather(tokens, "tp", axis=1, tiled=True)

    kv_parts = []
    for step in range(groups):
        part = jnp.concatenate([columns(keys, step), columns(values, step)], axis=0)
        if step == 0:
            part, _ = lax.optimization_barrier((part, after_halving))
        elif step < groups - 1:
            part, _ = lax.optimization_barrier((part, fetched))
        if step:
            part = swap(part, step * ranks)
        have = {0: part}
        bit = ranks // 2
        while bit:
            have.update({j | bit: swap(x, bit) for j, x in list(have.items())})
            bit //= 2
        kv_parts += [have[j] for j in range(ranks)]

    features = whole.astype(jnp.float32)
    mean_square = jnp.mean(features * features, axis=-1, keepdims=True)
    normed = (features * lax.rsqrt(mean_square + norm_eps) * gain.astype(jnp.float32)).astype(
        jnp.bfloat16
    )
    query_merged = merge_weight(query_frozen_weight, query_down_t, query_up)
    queries = jnp.dot(normed, query_merged, preferred_element_type=jnp.float32).astype(jnp.bfloat16)

    q_parts = []
    for step in range(groups):
        part = columns(queries, step)
        q_parts.append(swap(part, step * ranks) if step else part)

    out_down_t, out_up, _, _ = fetch_pair(
        output_update_first[0], output_update_second[0], owners[2], owners[3], hold=queries
    )
    out_merged = merge_weight(output_frozen_weight, out_down_t, out_up)

    order = list(range(1, groups)) + [0]
    o_parts = [None] * groups
    gate = None
    for step in order:
        q_part = q_parts[step]
        if gate is not None:
            q_part, _ = lax.optimization_barrier((q_part, gate))
        gate = attend(q_part, kv_parts, (my_group ^ step) * ranks + me % ranks, frame_block_number)
        o_parts[step] = swap(gate, step * ranks) if step else gate
    stacked = jnp.stack(o_parts)
    attended = jnp.concatenate(
        [lax.dynamic_index_in_dim(stacked, my_group ^ g, 0, keepdims=False) for g in range(groups)],
        axis=1,
    )
    if tp != 2:
        partial_value = jnp.dot(attended, out_merged, preferred_element_type=jnp.float32)
        return lax.psum_scatter(
            partial_value.astype(jnp.bfloat16), "tp", scatter_dimension=1, tiled=True
        )
    half = out_merged.shape[1] // 2
    pieces = 4
    step = half // pieces
    received = []
    for i in range(pieces):
        theirs = lax.dynamic_slice_in_dim(out_merged, (1 - mine) * half + i * step, step, 1)
        product = jnp.dot(attended, theirs, preferred_element_type=jnp.float32)
        received.append(lax.ppermute(product.astype(jnp.bfloat16), "tp", [(0, 1), (1, 0)]))
    own = lax.dynamic_slice_in_dim(out_merged, mine * half, half, 1)
    product = jnp.dot(attended, own, preferred_element_type=jnp.float32)
    return jnp.concatenate(
        [
            (product[:, i * step : (i + 1) * step] + received[i].astype(jnp.float32)).astype(
                jnp.bfloat16
            )
            for i in range(pieces)
        ],
        axis=1,
    )


def solution(mesh):
    in_specs = (
        P("ctx", "tp"),
        P("tp"),
        P("ctx", "tp"),
        P("ctx", "tp"),
        P(None, "tp"),
        P("tp", None),
        P("ctx", None, None),
        P("ctx", None, "tp"),
        P("ctx", "tp", None),
        P("ctx", None, None),
        P(),
        P(),
    )
    out_specs = P("ctx", "tp")
    return jax.shard_map(shards, mesh=mesh, in_specs=in_specs, out_specs=out_specs, check_vma=False)
```
